32 devices in a mesh: groups: 2 (over y), blk: 4 (over z), rhs: 2 (over x), sub: 2 (over core).
Axes of the slice: x: 2, y: 2, z: 4, core: 2. Of those that a mesh axis runs over, the one named last changes fastest.
Arguments:
- coords: bfloat16 [64, 16384], P(None, ('groups', 'blk')), parts along dimension 1, may hold values from -1.5 to 1.5
- values: bfloat16 [64, 16384], P('rhs', ('groups', 'blk')), parts along dimension 1, may hold values from -6 to 6
- tree_order: int32 [16384], P(('groups', 'blk')), parts along dimension 0, may hold values from 0 to 8191, as said below
- near_mask: int32 [8, 2], P(('groups', 'blk')), parts along dimension 0, may hold values 0 or 1
- skel_leaf: int32 [8, 256], P(('groups', 'blk')), parts along dimension 0, may hold values from 0 to 2047, as said below
- skel_up: int32 [4, 256], P('groups'), parts along dimension 0, may hold values from 0 to 511, as said below
Outputs:
- product: float32 [64, 8, 2048], P('rhs', ('groups', 'blk'), 'sub'), parts along dimension 1
The draws below stay inside these ranges and needn't reach their ends.
There are 2 independent parts, one for each index of `groups`. The reference program is written for one: setup_inputs(seed, part) draws one part's arguments, and reference() takes and returns one part's arrays. A program takes and returns all parts, laid end to end along the dimension named above; each array names one. Nothing has to cross between parts.
Inputs may be any that keep to these rules, and one draw needn't show every extreme that they name: Each sample appears once, and position p and sample tree_order[p] lie in the same span of 2048 positions. `skel_leaf`: each row holds 256 different row numbers within its leaf. `skel_up`: each row holds 256 different positions among the 512 skeleton samples of the node's two children, the left child's first.
All inputs are finite; a program needn't handle non-finite values. No bound on the sum of `near_mask` on one device may be relied on, other than what follows from the above.
Results may differ from the reference program's by a relative error of at most 0.00075.
Values may be sent and summed in bfloat16 or wider, within the bound.
A program may use at most 64 MiB of HBM per device.

```python
import jax
import jax.numpy as jnp
from jax import lax

DIM = 64
RHS = 64
B = 2048
R = 256
LEAF_DEV = 1
LEAVES = 4
SAMPLES = 8192
NODES = 2


def shifted_rows(key, row_total, choose, span_size):
    row_keys = jax.random.split(key, row_total)
    shuffled = jax.vmap(lambda one_key: jax.random.permutation(one_key, span_size))(row_keys)[:, :choose]
    first_shift = jnp.where(jnp.arange(row_total) == 0, span_size - 1 - shuffled[:, 0], 0)
    return ((shuffled + first_shift[:, None]) % span_size).astype(jnp.int32)


def draw_tree_order(key, part):
    key = jax.random.fold_in(key, 3)
    span_size = LEAF_DEV * B
    block_count = SAMPLES // span_size
    block_keys = jax.random.split(key, block_count)
    shuffled = jax.vmap(lambda one_key: jax.random.permutation(one_key, span_size))(block_keys)
    shifted = shuffled + jnp.arange(block_count)[:, None] * span_size
    return shifted.reshape(-1).astype(jnp.int32)


def draw_skel_leaf(key, part):
    key = jax.random.fold_in(key, 5)
    return shifted_rows(key, LEAVES, R, B)


def draw_skel_up(key, part):
    key = jax.random.fold_in(key, 7)
    return shifted_rows(key, NODES, R, 2 * R)


def set_ends(drawn, key, smallest, top_value):
    dims = drawn.shape
    index_at = [jax.random.randint(jax.random.fold_in(key, axis), (), 0, dims[axis]) for axis in range(len(dims))]
    drawn = drawn.at[tuple(index_at)].set(smallest)
    longest = dims.index(max(dims))
    index_at[longest] = (index_at[longest] + 1) % dims[longest]
    return drawn.at[tuple(index_at)].set(top_value)


def shard_levels(key, extent, cuts, least, top_value):
    gain, own = 1.0, jax.random.fold_in(key, 6)
    for position, parts in cuts:
        heights = jnp.exp(jax.random.uniform(jax.random.fold_in(own, position), (parts,), jnp.float32, least / len(cuts), top_value / len(cuts)))
        gain = gain * jnp.repeat(heights, extent[position] // parts).reshape([-1 if axis == position else 1 for axis in range(len(extent))])
    return gain


def noise(stream_key, extent, deviation, most, cuts=(), held_as=jnp.bfloat16):
    result = jax.random.normal(stream_key, extent, jnp.float32) * deviation
    if len(cuts) > 0:
        result = shard_levels(stream_key, extent, cuts, -0.22, 0.18) * result
    return jnp.clip(result, min=-most, max=most).astype(held_as)


def setup_inputs(seed: int = 0, part: int = 0) -> dict:
    streams_of = jax.random.split(jax.random.key(seed), 7)
    part_splits = jax.random.split(jax.random.fold_in(streams_of[6], part), 7)
    return {
        "coords": noise(part_splits[0], (DIM, SAMPLES), 0.25, 1.5, ((1, 4),)),
        "values": noise(part_splits[1], (RHS, SAMPLES), 1.0, 6.0, ((0, 2), (1, 4))),
        "tree_order": draw_tree_order(jax.random.fold_in(jax.random.fold_in(streams_of[6], part), 71), part),
        "near_mask": set_ends((jax.random.randint(part_splits[3], (LEAVES, 2), 0, 2) < 1).astype(jnp.int32), jax.random.fold_in(part_splits[3], 1), 0, 1),
        "skel_leaf": draw_skel_leaf(jax.random.fold_in(jax.random.fold_in(streams_of[6], part), 71), part),
        "skel_up": draw_skel_up(jax.random.fold_in(jax.random.fold_in(streams_of[6], part), 71), part),
    }


def kernel(targets, sources):
    sharpness = 32.0 / targets.shape[0]
    products = lax.dot_general(targets, sources, (((0,), (0,)), ((), ())), preferred_element_type=jnp.float32)
    target_sq = jnp.sum(jnp.square(targets.astype(jnp.float32)), axis=0)
    source_sq = jnp.sum(jnp.square(sources.astype(jnp.float32)), axis=0)
    return jnp.exp(-sharpness * (target_sq[:, None] + source_sq[None, :] - 2.0 * products)).astype(jnp.bfloat16)


def apply_tile(weights, tile_values):
    return lax.dot_general(weights, tile_values, (((1,), (1,)), ((), ())), preferred_element_type=jnp.float32)


def pair_up(level_packs):
    node_count, height, skeleton = level_packs.shape
    joined = level_packs.reshape(node_count // 2, 2, height, skeleton).transpose(0, 2, 1, 3)
    return joined.reshape(node_count // 2, height, 2 * skeleton)


def merge_children(pair_packs, chosen_rows, features):
    parents_z = jax.vmap(lambda packed, chosen: jnp.take(packed[:features], chosen, axis=1))(pair_packs, chosen_rows)

    def weigh_node(packed, parent):
        return apply_tile(packed[features:], kernel(parent, packed[:features])).astype(jnp.bfloat16)

    parents_w = jax.vmap(weigh_node)(pair_packs, parents_z)
    return jnp.concatenate([parents_z, parents_w], axis=1)


def reference(coords, values, tree_order, near_mask, skel_leaf, skel_up):
    tree_coords = jnp.take(coords, tree_order, axis=1)
    tree_values = jnp.take(values, tree_order, axis=1)
    leaf_coords = tree_coords.reshape(DIM, LEAVES, B).transpose(1, 0, 2)
    leaf_values = tree_values.reshape(RHS, LEAVES, B).transpose(1, 0, 2)

    def near_leaf(leaf_index):
        targets = leaf_coords[leaf_index]

        def near_pair(partner):
            return apply_tile(leaf_values[partner], kernel(targets, leaf_coords[partner]))

        summed = near_pair(leaf_index)
        summed = summed + near_mask[leaf_index, 0].astype(jnp.float32) * near_pair(leaf_index ^ 1)
        summed = summed + near_mask[leaf_index, 1].astype(jnp.float32) * (near_pair(leaf_index ^ 2) + near_pair(leaf_index ^ 3))
        return summed

    near_terms = lax.map(near_leaf, jnp.arange(LEAVES, dtype=jnp.int32))

    def leaf_node(leaf_x, leaf_v, chosen):
        skeleton_z = jnp.take(leaf_x, chosen, axis=1)
        weights = apply_tile(leaf_v, kernel(skeleton_z, leaf_x)).astype(jnp.bfloat16)
        return jnp.concatenate([skeleton_z, weights], axis=0)

    level_packs = [jax.vmap(leaf_node)(leaf_coords, leaf_values, skel_leaf)]
    levels = LEAVES.bit_length() - 1
    for level_number in range(1, levels):
        first_row = LEAVES - (LEAVES >> (level_number - 1))
        node_count = LEAVES >> level_number
        level_packs.append(merge_children(pair_up(level_packs[-1]), skel_up[first_row:first_row + node_count], DIM))

    def far_leaf(leaf_index):
        pieces = []
        for level_number in range(levels):
            packed = lax.dynamic_index_in_dim(level_packs[level_number], (leaf_index >> level_number) ^ 1, 0, keepdims=False)
            if level_number < 2:
                factor = (1 - near_mask[leaf_index, level_number]).astype(jnp.bfloat16)
                packed = jnp.concatenate([packed[:DIM], packed[DIM:] * factor], axis=0)
            pieces.append(packed)
        packed = jnp.concatenate(pieces, axis=1)
        return apply_tile(packed[DIM:], kernel(leaf_coords[leaf_index], packed[:DIM]))

    far_terms = lax.map(far_leaf, jnp.arange(LEAVES, dtype=jnp.int32))
    return (near_terms + far_terms).transpose(1, 0, 2)
```

```python
import functools

import jax
import jax.numpy as jnp
from jax import lax
from jax.experimental import pallas as pl
from jax.experimental.pallas import tpu as pltpu
from jax.sharding import PartitionSpec as P

MESH = pl.DeviceIdType.MESH
DEPTH = 128
CHUNK = 256


def norm_rows(x, is_source, features):
    wide = x.astype(jnp.float32)
    norm = (-32.0 / features) * jnp.sum(wide * wide, axis=0, keepdims=True)
    high = norm.astype(jnp.bfloat16).astype(jnp.float32)
    rest = norm - high
    middle = rest.astype(jnp.bfloat16).astype(jnp.float32)
    low = rest - middle
    row = lax.broadcasted_iota(jnp.int32, (16, x.shape[1]), 0)
    first = 0 if is_source else 3
    ones = (row >= 3 - first) & (row < 6 - first)
    rows = jnp.where(ones, 1.0, 0.0)
    for place, part in enumerate((high, middle, low)):
        rows = jnp.where(row == first + place, part, rows)
    return rows.astype(jnp.bfloat16)


def augmented(x, is_source):
    features, count = x.shape
    scaled = x if is_source else (x.astype(jnp.float32) * (64.0 / features)).astype(jnp.bfloat16)
    pad = jnp.zeros((DEPTH - features - 16, count), jnp.bfloat16)
    return jnp.concatenate([scaled, norm_rows(x, is_source, features), pad], axis=0)


def one_hot(count, first, index):
    row = lax.broadcasted_iota(jnp.int32, (count, index.shape[1]), 0) + first
    return jnp.where(row == index, 1.0, 0.0).astype(jnp.bfloat16)


def dot(left, right):
    return jnp.dot(left, right, preferred_element_type=jnp.float32)


def body(
    sizes,
    coords,
    values,
    order,
    mask,
    skel,
    skel_up,
    out,
    xs,
    vs,
    packs,
    sibs,
    src_t,
    scaled,
    tgt,
    z_send,
    z_recv,
    f_send,
    f_recv,
    p_send,
    p_recv,
):
    blk_size, sub_size = sizes
    features, rows = coords.shape
    skeleton = skel.shape[1]
    half = rows // sub_size
    bits = blk_size.bit_length() - 1
    total_leaves = skel_up.shape[0] + 2
    blk = lax.axis_index("blk")
    rhs = lax.axis_index("rhs")
    sub = lax.axis_index("sub")

    def flip(number, bit):
        return number + bit - 2 * bit * ((number // bit) % 2)

    across = flip(rhs, 1)
    other = 1 - sub
    near_1, near_2 = {"blk": flip(blk, 1)}, {"blk": flip(blk, 2)}
    chip_mates = [{"rhs": across}, {"sub": other}, {"rhs": across, "sub": other}]
    partners = [near_1, near_2] + chip_mates
    partners += [{"blk": flip(blk, 2**bit)} for bit in range(2, bits)]

    barrier = pltpu.get_barrier_semaphore()
    for partner in partners:
        pl.semaphore_signal(barrier, inc=1, device_id=partner, device_id_type=MESH)
    pl.semaphore_wait(barrier, len(partners))

    share = features // 4
    quarter = pl.ds(pl.multiple_of((sub * 2 + rhs % 2) * share, share), share)
    lanes = pl.ds(pl.multiple_of(sub * half, half), half)

    def remote(source, target, send, recv, partner):
        return pltpu.make_async_remote_copy(
            src_ref=source,
            dst_ref=target,
            send_sem=send,
            recv_sem=recv,
            device_id=partner,
            device_id_type=MESH,
        )

    def far_copies(slot, from_x, from_v, partner):
        return [
            remote(from_x.at[quarter], xs.at[slot, quarter], z_send.at[slot, 0], z_recv.at[slot, 0], partner),
            remote(
                from_v.at[:, lanes], vs.at[slot, :, lanes], z_send.at[slot, 1], z_recv.at[slot, 1], partner
            ),
        ]

    hops = [far_copies(0, coords, values, near_1), far_copies(1, coords, values, near_2)]
    hops.append(far_copies(2, xs.at[1], vs.at[1], near_1))

    def spread_copies(slot):
        found = [
            remote(
                xs.at[slot, quarter],
                xs.at[slot, quarter],
                f_send.at[slot, place],
                f_recv.at[slot, place],
                mate,
            )
            for place, mate in enumerate(chip_mates)
        ]
        block = vs.at[slot, :, lanes]
        found.append(remote(block, block, f_send.at[slot, 3], f_recv.at[slot, 3], chip_mates[1]))
        return found

    spreads = [spread_copies(slot) for slot in range(3)]
    pack_copies = [
        remote(packs.at[bit], sibs.at[bit], p_send.at[bit], p_recv.at[bit], {"blk": flip(blk, 2**bit)})
        for bit in range(bits)
    ]

    def start(copies):
        for copy in copies:
            copy.start()

    def arrive(copies):
        for copy in copies:
            copy.wait_recv()

    start(hops[0])
    start(hops[1])

    local = order[...] - blk * rows
    own = coords[...]
    mine = order[:, lanes] - blk * rows
    skel_hot = one_hot(rows, 0, skel[...])
    digits = jnp.concatenate([local // 256, local % 256], axis=0).astype(jnp.float32)
    digits = jnp.concatenate([digits, jnp.zeros((14, rows), jnp.float32)], axis=0).astype(jnp.bfloat16)
    places = dot(digits, skel_hot)
    skel_rows = (places[0:1] * 256.0 + places[1:2]).astype(jnp.int32)
    src_t[0] = augmented(own, True).T

    def gathered(pieces, index):
        total = None
        for piece, first in pieces:
            term = dot(piece, one_hot(piece.shape[1], first, index))
            total = term if total is None else total + term
        return total.astype(jnp.bfloat16)

    pieces = [(own[:, first : first + 512], first) for first in range(0, rows, 512)]
    z = gathered(pieces, skel_rows)
    z_tgt = augmented(z, False)
    total = jnp.zeros((values.shape[0], skeleton), jnp.float32)
    for first in range(0, rows, 512):
        tile = jnp.exp(dot(src_t[0, first : first + 512], z_tgt)).astype(jnp.bfloat16)
        total = total + dot(values[:, first : first + 512], tile)
    packs[0, :features] = z
    packs[0, features:] = total.astype(jnp.bfloat16)
    pack_copies[0].start()
    tgt[...] = augmented(gathered(pieces, mine), False)

    arrive(hops[0])
    start(spreads[0])

    out[...] = jnp.zeros_like(out)

    def near(slot, weights):
        def step(index, carry):
            at = pl.ds(pl.multiple_of(index * CHUNK, CHUNK), CHUNK)
            tile = jnp.exp(dot(src_t[slot, at], tgt[...])).astype(jnp.bfloat16)
            out[...] += dot(weights[:, at], tile)
            return carry

        lax.fori_loop(0, rows // CHUNK, step, 0)

    near(0, values)

    arrive(hops[1])
    start(hops[2])
    start(spreads[1])

    def near_slot(slot, column):
        arrive(spreads[slot])
        src_t[slot + 1] = augmented(xs[slot], True).T
        factor = mask[0, column].astype(jnp.float32)
        scaled[slot] = (vs[slot].astype(jnp.float32) * factor).astype(jnp.bfloat16)
        near(slot + 1, scaled.at[slot])

    def merge(bit):
        on_right = (blk // 2**bit) % 2
        first_row = total_leaves - (total_leaves >> bit) + blk // 2 ** (bit + 1)
        chosen = skel_up[pl.ds(first_row, 1)]
        pack_copies[bit].wait_recv()
        mine_z, other_z = packs[bit, :features], sibs[bit, :features]
        parent = gathered(
            [(mine_z, on_right * skeleton), (other_z, (1 - on_right) * skeleton)], chosen
        )
        parent_tgt = augmented(parent, False)
        summed = None
        for pack, side in ((packs, mine_z), (sibs, other_z)):
            tile = jnp.exp(dot(augmented(side, True).T, parent_tgt)).astype(jnp.bfloat16)
            term = dot(pack[bit, features:], tile)
            summed = term if summed is None else summed + term
        packs[bit + 1, :features] = parent
        packs[bit + 1, features:] = summed.astype(jnp.bfloat16)
        pack_copies[bit + 1].start()

    near_slot(0, 0)
    merge(0)
    arrive(hops[2])
    start(spreads[2])
    near_slot(1, 1)
    for bit in range(1, bits - 1):
        merge(bit)
    near_slot(2, 1)
    pack_copies[bits - 1].wait_recv()
    for bit in range(bits):
        weights = sibs[bit, features:]
        if bit < 2:
            factor = (1 - mask[0, bit]).astype(jnp.float32)
            weights = (weights.astype(jnp.float32) * factor).astype(jnp.bfloat16)
        tile = jnp.exp(dot(augmented(sibs[bit, :features], True).T, tgt[...])).astype(jnp.bfloat16)
        out[...] += dot(weights, tile)

    for copies in hops + spreads + [pack_copies]:
        for copy in copies:
            copy.wait_send()


def shards(mesh, coords, values, tree_order, near_mask, skel_leaf, skel_up):
    features, rows = coords.shape
    columns = values.shape[0]
    skeleton = skel_leaf.shape[1]
    sub_size = mesh.shape["sub"]
    bits = mesh.shape["blk"].bit_length() - 1
    half = rows // sub_size
    held = max(columns, 16)
    if held > columns:
        values = jnp.pad(values, ((0, held - columns), (0, 0)))
    vmem = pl.BlockSpec(memory_space=pltpu.VMEM)
    result = pl.pallas_call(
        functools.partial(body, (mesh.shape["blk"], sub_size)),
        out_shape=jax.ShapeDtypeStruct((held, half), jnp.float32),
        in_specs=[vmem, vmem, vmem, pl.BlockSpec(memory_space=pltpu.SMEM), vmem, vmem],
        out_specs=vmem,
        scratch_shapes=[
            pltpu.VMEM((3, features, rows), jnp.bfloat16),
            pltpu.VMEM((3, held, rows), jnp.bfloat16),
            pltpu.VMEM((bits, features + held, skeleton), jnp.bfloat16),
            pltpu.VMEM((bits, features + held, skeleton), jnp.bfloat16),
            pltpu.VMEM((4, rows, DEPTH), jnp.bfloat16),
            pltpu.VMEM((3, held, rows), jnp.bfloat16),
            pltpu.VMEM((DEPTH, half), jnp.bfloat16),
            pltpu.SemaphoreType.DMA((3, 2)),
            pltpu.SemaphoreType.DMA((3, 2)),
            pltpu.SemaphoreType.DMA((3, 4)),
            pltpu.SemaphoreType.DMA((3, 4)),
            pltpu.SemaphoreType.DMA((bits,)),
            pltpu.SemaphoreType.DMA((bits,)),
        ],
        compiler_params=pltpu.CompilerParams(
            collective_id=0, has_side_effects=True, vmem_limit_bytes=48 * 2**20
        ),
    )(coords, values, tree_order.reshape(1, rows), near_mask, skel_leaf, skel_up)
    return result[:columns].reshape(columns, 1, half)


def solution(mesh):
    return jax.shard_map(
        functools.partial(shards, mesh),
        mesh=mesh,
        in_specs=(
            P(None, ("groups", "blk")),
            P("rhs", ("groups", "blk")),
            P(("groups", "blk")),
            P(("groups", "blk"), None),
            P(("groups", "blk"), None),
            P("groups", None),
        ),
        out_specs=P("rhs", ("groups", "blk"), "sub"),
        check_vma=False,
    )
```

```python
import functools

import jax
import jax.numpy as jnp
from jax import lax
from jax.experimental import pallas as pl
from jax.experimental.pallas import tpu as pltpu
from jax.sharding import PartitionSpec as P

MESH = pl.DeviceIdType.MESH
DEPTH = 128
TARGETS = 512


def norm_rows(x, is_source, features):
    wide = x.astype(jnp.float32)
    norm = (-32.0 / features) * jnp.sum(wide * wide, axis=0, keepdims=True)
    high = norm.astype(jnp.bfloat16).astype(jnp.float32)
    rest = norm - high
    middle = rest.astype(jnp.bfloat16).astype(jnp.float32)
    low = rest - middle
    row = lax.broadcasted_iota(jnp.int32, (16, x.shape[1]), 0)
    first = 0 if is_source else 3
    ones = (row >= 3 - first) & (row < 6 - first)
    rows = jnp.where(ones, 1.0, 0.0)
    for place, part in enumerate((high, middle, low)):
        rows = jnp.where(row == first + place, part, rows)
    return rows.astype(jnp.bfloat16)


def augmented(x, is_source):
    features, count = x.shape
    scaled = x if is_source else (x.astype(jnp.float32) * (64.0 / features)).astype(jnp.bfloat16)
    pad = jnp.zeros((DEPTH - features - 16, count), jnp.bfloat16)
    return jnp.concatenate([scaled, norm_rows(x, is_source, features), pad], axis=0)


def one_hot(count, first, index):
    row = lax.broadcasted_iota(jnp.int32, (count, index.shape[1]), 0) + first
    return jnp.where(row == index, 1.0, 0.0).astype(jnp.bfloat16)


def dot(left, right):
    return jnp.dot(left, right, preferred_element_type=jnp.float32)


def body(
    sizes,
    coords_hbm,
    values_hbm,
    order_hbm,
    mask_hbm,
    skel_hbm,
    skel_up_hbm,
    result,
    coords,
    values,
    order,
    mask,
    skel,
    skel_up,
    out,
    xs,
    vs,
    packs,
    sibs,
    src_t,
    scaled,
    tgt,
    z_send,
    z_recv,
    f_send,
    f_recv,
    p_send,
    p_recv,
    local_sems,
):
    blk_size, sub_size = sizes
    features, rows = coords.shape
    skeleton = skel.shape[1]
    half = rows // sub_size
    bits = blk_size.bit_length() - 1
    total_leaves = skel_up.shape[0] + 2
    blk = lax.axis_index("blk")
    rhs = lax.axis_index("rhs")
    sub = lax.axis_index("sub")

    def start_all(copies):
        for copy in copies:
            copy.start()

    def flip(number, bit):
        return number + bit - 2 * bit * ((number // bit) % 2)

    across = flip(rhs, 1)
    other = 1 - sub
    near_1, near_2 = {"blk": flip(blk, 1)}, {"blk": flip(blk, 2)}
    chip_mates = [{"rhs": across}, {"sub": other}, {"rhs": across, "sub": other}]
    partners = [near_1, near_2] + chip_mates
    partners += [{"blk": flip(blk, 2**bit)} for bit in range(2, bits)]

    loads = [
        pltpu.make_async_copy(source, target, local_sems.at[place])
        for place, (source, target) in enumerate(
            [
                (order_hbm, order),
                (skel_hbm, skel),
                (coords_hbm, coords),
                (values_hbm, values),
                (skel_up_hbm, skel_up),
                (mask_hbm, mask),
            ]
        )
    ]
    barrier = pltpu.get_barrier_semaphore()
    for partner in partners:
        pl.semaphore_signal(barrier, inc=1, device_id=partner, device_id_type=MESH)
    start_all(loads)
    pl.semaphore_wait(barrier, len(partners))

    share = features // 4
    quarter = pl.ds(pl.multiple_of((sub * 2 + rhs % 2) * share, share), share)
    lanes = pl.ds(pl.multiple_of(sub * half, half), half)

    def remote(source, target, send, recv, partner):
        return pltpu.make_async_remote_copy(
            src_ref=source,
            dst_ref=target,
            send_sem=send,
            recv_sem=recv,
            device_id=partner,
            device_id_type=MESH,
        )

    def far_copies(slot, from_x, from_v, partner):
        return [
            remote(from_x.at[quarter], xs.at[slot, quarter], z_send.at[slot, 0], z_recv.at[slot, 0], partner),
            remote(
                from_v.at[:, lanes], vs.at[slot, :, lanes], z_send.at[slot, 1], z_recv.at[slot, 1], partner
            ),
        ]

    hops = [far_copies(0, coords_hbm, values_hbm, near_1), far_copies(1, coords_hbm, values_hbm, near_2)]
    hops.append(far_copies(2, xs.at[1], vs.at[1], near_1))

    def spread_copies(slot):
        found = [
            remote(
                xs.at[slot, quarter],
                xs.at[slot, quarter],
                f_send.at[slot, place],
                f_recv.at[slot, place],
                mate,
            )
            for place, mate in enumerate(chip_mates)
        ]
        block = vs.at[slot, :, lanes]
        found.append(remote(block, block, f_send.at[slot, 3], f_recv.at[slot, 3], chip_mates[1]))
        return found

    spreads = [spread_copies(slot) for slot in range(3)]
    pack_copies = [
        remote(packs.at[bit], sibs.at[bit], p_send.at[bit], p_recv.at[bit], {"blk": flip(blk, 2**bit)})
        for bit in range(bits)
    ]

    def arrive(copies):
        for copy in copies:
            copy.wait_recv()

    start_all(hops[1])
    start_all(hops[0])

    for load in loads:
        load.wait()

    local = order[...] - blk * rows
    own = coords[...]
    mine = order[:, lanes] - blk * rows
    skel_hot = one_hot(rows, 0, skel[...])
    digits = jnp.concatenate([local // 256, local % 256], axis=0).astype(jnp.float32)
    digits = jnp.concatenate([digits, jnp.zeros((14, rows), jnp.float32)], axis=0).astype(jnp.bfloat16)
    places = dot(digits, skel_hot)
    skel_rows = (places[0:1] * 256.0 + places[1:2]).astype(jnp.int32)
    src_t[0] = augmented(own, True).T

    def gathered(pieces, index):
        total = None
        for piece, first in pieces:
            term = dot(piece, one_hot(piece.shape[1], first, index))
            total = term if total is None else total + term
        return total.astype(jnp.bfloat16)

    pieces = [(own[:, first : first + 512], first) for first in range(0, rows, 512)]
    z = gathered(pieces, skel_rows)
    z_tgt = augmented(z, False)
    total = jnp.zeros((values.shape[0], skeleton), jnp.float32)
    for first in range(0, rows, 512):
        tile = jnp.exp(dot(src_t[0, first : first + 512], z_tgt)).astype(jnp.bfloat16)
        total = total + dot(values[:, first : first + 512], tile)
    packs[0, :features] = z
    packs[0, features:] = total.astype(jnp.bfloat16)
    pack_copies[0].start()
    tgt[...] = augmented(gathered(pieces, mine), False)

    arrive(hops[0])
    start_all(spreads[0])

    out[...] = jnp.zeros_like(out)

    def near(slot, weights):
        for first in range(0, half, TARGETS):
            at = pl.ds(first, TARGETS)
            tile = jnp.exp(dot(src_t[slot], tgt[:, at])).astype(jnp.bfloat16)
            out[:, at] += dot(weights[...], tile)

    near(0, values)

    arrive(hops[1])
    start_all(hops[2])
    start_all(spreads[1])

    def near_slot(slot, column):
        arrive(spreads[slot])
        src_t[slot + 1] = augmented(xs[slot], True).T
        factor = mask[0:1, column : column + 1].astype(jnp.float32)
        scaled[slot] = (vs[slot].astype(jnp.float32) * factor).astype(jnp.bfloat16)
        near(slot + 1, scaled.at[slot])

    def merge(bit):
        on_right = (blk // 2**bit) % 2
        first_row = total_leaves - (total_leaves >> bit) + blk // 2 ** (bit + 1)
        chosen = skel_up[pl.ds(first_row, 1)]
        pack_copies[bit].wait_recv()
        mine_z, other_z = packs[bit, :features], sibs[bit, :features]
        parent = gathered(
            [(mine_z, on_right * skeleton), (other_z, (1 - on_right) * skeleton)], chosen
        )
        parent_tgt = augmented(parent, False)
        summed = None
        for pack, side in ((packs, mine_z), (sibs, other_z)):
            tile = jnp.exp(dot(augmented(side, True).T, parent_tgt)).astype(jnp.bfloat16)
            term = dot(pack[bit, features:], tile)
            summed = term if summed is None else summed + term
        packs[bit + 1, :features] = parent
        packs[bit + 1, features:] = summed.astype(jnp.bfloat16)
        pack_copies[bit + 1].start()

    near_slot(0, 0)
    merge(0)
    arrive(hops[2])
    start_all(spreads[2])
    near_slot(1, 1)
    for bit in range(1, bits - 1):
        merge(bit)
    near_slot(2, 1)
    pack_copies[bits - 1].wait_recv()
    for bit in range(bits):
        weights = sibs[bit, features:]
        if bit < 2:
            factor = (1 - mask[0:1, bit : bit + 1]).astype(jnp.float32)
            weights = (weights.astype(jnp.float32) * factor).astype(jnp.bfloat16)
        tile = jnp.exp(dot(augmented(sibs[bit, :features], True).T, tgt[...])).astype(jnp.bfloat16)
        out[...] += dot(weights, tile)

    store = pltpu.make_async_copy(out.at[: result.shape[0]], result.at[:, 0], local_sems.at[6])
    store.start()
    for copies in hops + spreads + [pack_copies]:
        for copy in copies:
            copy.wait_send()
    store.wait()


def shards(mesh, coords, values, tree_order, near_mask, skel_leaf, skel_up):
    features, rows = coords.shape
    columns = values.shape[0]
    skeleton = skel_leaf.shape[1]
    sub_size = mesh.shape["sub"]
    bits = mesh.shape["blk"].bit_length() - 1
    half = rows // sub_size
    held = max(columns, 16)
    if held > columns:
        values = jnp.pad(values, ((0, held - columns), (0, 0)))
    hbm = pl.BlockSpec(memory_space=pltpu.HBM)
    return pl.pallas_call(
        functools.partial(body, (mesh.shape["blk"], sub_size)),
        out_shape=jax.ShapeDtypeStruct((columns, 1, half), jnp.float32),
        in_specs=[hbm] * 6,
        out_specs=hbm,
        scratch_shapes=[
            pltpu.VMEM((features, rows), jnp.bfloat16),
            pltpu.VMEM((held, rows), jnp.bfloat16),
            pltpu.VMEM((1, rows), jnp.int32),
            pltpu.VMEM((1, 2), jnp.int32),
            pltpu.VMEM((1, skeleton), jnp.int32),
            pltpu.VMEM(skel_up.shape, jnp.int32),
            pltpu.VMEM((held, half), jnp.float32),
            pltpu.VMEM((3, features, rows), jnp.bfloat16),
            pltpu.VMEM((3, held, rows), jnp.bfloat16),
            pltpu.VMEM((bits, features + held, skeleton), jnp.bfloat16),
            pltpu.VMEM((bits, features + held, skeleton), jnp.bfloat16),
            pltpu.VMEM((4, rows, DEPTH), jnp.bfloat16),
            pltpu.VMEM((3, held, rows), jnp.bfloat16),
            pltpu.VMEM((DEPTH, half), jnp.bfloat16),
            pltpu.SemaphoreType.DMA((3, 2)),
            pltpu.SemaphoreType.DMA((3, 2)),
            pltpu.SemaphoreType.DMA((3, 4)),
            pltpu.SemaphoreType.DMA((3, 4)),
            pltpu.SemaphoreType.DMA((bits,)),
            pltpu.SemaphoreType.DMA((bits,)),
            pltpu.SemaphoreType.DMA((7,)),
        ],
        compiler_params=pltpu.CompilerParams(
            collective_id=0, has_side_effects=True, vmem_limit_bytes=60 * 2**20
        ),
    )(coords, values, tree_order.reshape(1, rows), near_mask, skel_leaf, skel_up)


def solution(mesh):
    return jax.shard_map(
        functools.partial(shards, mesh),
        mesh=mesh,
        in_specs=(
            P(None, ("groups", "blk")),
            P("rhs", ("groups", "blk")),
            P(("groups", "blk")),
            P(("groups", "blk"), None),
            P(("groups", "blk"), None),
            P("groups", None),
        ),
        out_specs=P("rhs", ("groups", "blk"), "sub"),
        check_vma=False,
    )
```
